32 devices in a mesh: wide: 8 (over y, x, core), narrow: 4 (over z).
Axes of the slice: x: 2, y: 2, z: 4, core: 2. Of those that a mesh axis runs over, the one named last changes fastest.
Arguments:
- constraint_rows: bfloat16 [512, 32, 1024], P(None, ('wide', 'narrow')), may hold values from -1 to 1
- metric: bfloat16 [1024, 1024], replicated, may hold values from -8 to 8, as said below
Outputs:
- factored: float32 [512, 32, 4, 256], P(None, 'wide', 'narrow')
The draws below stay inside these ranges and needn't reach their ends.
Inputs may be any that keep to these rules, and one draw needn't show every extreme that they name: `metric`: symmetric and positive definite.
All inputs are finite; a program needn't handle non-finite values.
Results may differ from the reference program's by a relative error of at most 0.0052.
Values may be sent and summed in bfloat16 or wider, within the bound.
A program may use at most 64 MiB of HBM per device.

```python
import jax
import jax.numpy as jnp
from jax import lax

N = 1024
P_SIZE = 1024
PB = 256
NPANEL = 2
LOCAL = 512
GROUPS = 32
N_NARROW = 4


def draw_constraint_rows(key, part):
    key_common, key_noise, key_scale = jax.random.split(jax.random.fold_in(key, 31), 3)
    common = jax.random.normal(key_common, (N,), jnp.float32)
    noise_draw = jax.random.normal(key_noise, (LOCAL, GROUPS, N), jnp.float32)
    row_scale = jnp.exp(jax.random.uniform(key_scale, (LOCAL, GROUPS, 1), jnp.float32, -0.35, 0.35))
    drawn_rows = row_scale * (0.7 * common + 0.7 * noise_draw) / jnp.sqrt(jnp.float32(N))
    return jnp.clip(drawn_rows, -1.0, 1.0).astype(jnp.bfloat16)


def draw_metric(key, part):
    key_base, key_diag = jax.random.split(jax.random.fold_in(key, 47))
    base_draw = jax.random.normal(key_base, (N, N), jnp.float32)
    gram_part = jnp.dot(base_draw, base_draw.T) / (2.0 * N)
    diag_shift = jax.random.uniform(jax.random.fold_in(key_diag, 5), (N,), jnp.float32, 0.5, 1.5)
    matrix = 0.5 * (gram_part + gram_part.T) + jnp.diag(diag_shift)
    return jnp.clip(matrix, -8.0, 8.0).astype(jnp.bfloat16)


def setup_inputs(seed: int = 0) -> dict:
    splits = jax.random.split(jax.random.key(seed), 3)
    return {
        "constraint_rows": draw_constraint_rows(jax.random.fold_in(splits[2], 71), 0),
        "metric": draw_metric(jax.random.fold_in(splits[2], 71), 0),
    }


def left_solve(factor_low, right_side):
    return jax.scipy.linalg.solve_triangular(factor_low, right_side, lower=True)

def reference(constraint_rows, metric):
    flat_rows = constraint_rows.reshape(LOCAL * GROUPS, N)
    panel_vectors = flat_rows[:P_SIZE]
    projected = jnp.dot(flat_rows.astype(jnp.float32), metric.astype(jnp.float32), preferred_element_type=jnp.float32).astype(jnp.bfloat16)
    gram_cols = jnp.dot(projected.astype(jnp.float32), panel_vectors.T.astype(jnp.float32), preferred_element_type=jnp.float32)
    schur_slab = gram_cols * gram_cols
    for panel_number in range(NPANEL):
        col_begin = panel_number * PB
        col_end = col_begin + PB
        diag_block = schur_slab[col_begin:col_end, col_begin:col_end]
        factor_low = jnp.linalg.cholesky(diag_block)
        upper_part = left_solve(factor_low, schur_slab[col_begin:col_end, col_end:])
        column = left_solve(factor_low, schur_slab[:, col_begin:col_end].T).T
        trailing = schur_slab[:, col_end:] - jnp.dot(column, upper_part, precision=lax.Precision.HIGHEST)
        schur_slab = jnp.concatenate([schur_slab[:, :col_begin], column, trailing], axis=1)
    return schur_slab.reshape(LOCAL, GROUPS, P_SIZE // N_NARROW, N_NARROW).transpose(0, 1, 3, 2)
```

```python
import functools

import jax
import jax.numpy as jnp
from jax import lax
from jax.experimental import pallas as pl
from jax.experimental.pallas import tpu as pltpu
from jax.sharding import PartitionSpec as P

P_SIZE = 1024
PB = 256
NPANEL = 2
DONE = PB * NPANEL
MESH = pl.DeviceIdType.MESH


def gather_kernel(n_wide, n_narrow, own_ref, out_ref, own_sem, send_sem, recv_sem):
    w, z = lax.axis_index("wide"), lax.axis_index("narrow")
    mates = [lax.rem(w + 2 * i, n_wide) for i in range(1, n_wide // 2)]
    twin = w + 1 - 2 * lax.rem(w, 2)
    column = [lax.rem(z + i, n_narrow) for i in range(1, n_narrow)]

    barrier = pltpu.get_barrier_semaphore()
    partners = [(w, p) for p in column] + [(m, z) for m in mates] + [(twin, z)]
    for partner in partners:
        pl.semaphore_signal(barrier, inc=1, device_id=partner, device_id_type=MESH)
    pl.semaphore_wait(barrier, len(partners))

    sent = []

    def send(src, slot, target):
        copy = pltpu.make_async_remote_copy(
            src_ref=src,
            dst_ref=out_ref.at[slot],
            send_sem=send_sem.at[len(sent)],
            recv_sem=recv_sem.at[slot],
            device_id=target,
            device_id_type=MESH,
        )
        copy.start()
        sent.append(copy)

    def arrived(slot):
        pltpu.make_async_remote_copy(
            src_ref=own_ref,
            dst_ref=out_ref.at[slot],
            send_sem=send_sem.at[0],
            recv_sem=recv_sem.at[slot],
            device_id=(twin, z),
            device_id_type=MESH,
        ).wait_recv()

    me = w * n_narrow + z
    for p in column:
        send(own_ref, me, (w, p))
    for m in mates:
        send(own_ref, me, (m, z))
    send(own_ref, me, (twin, z))
    keep = pltpu.make_async_copy(own_ref, out_ref.at[me], own_sem)
    keep.start()
    for p in column:
        slot = w * n_narrow + p
        arrived(slot)
        for m in mates:
            send(out_ref.at[slot], slot, (m, z))
        send(out_ref.at[slot], slot, (twin, z))
    for p in [z] + column:
        for m in mates:
            slot = m * n_narrow + p
            arrived(slot)
            send(out_ref.at[slot], slot, (twin, z))
    for p in [z] + column:
        for m in [w] + mates:
            arrived((m + 1 - 2 * lax.rem(m, 2)) * n_narrow + p)
    keep.wait()
    for copy in sent:
        copy.wait_send()


def gather_panel(own, n_wide, n_narrow):
    groups = n_wide * n_narrow
    return pl.pallas_call(
        functools.partial(gather_kernel, n_wide, n_narrow),
        out_shape=jax.ShapeDtypeStruct((groups,) + own.shape, own.dtype),
        in_specs=[pl.BlockSpec(memory_space=pltpu.VMEM)],
        out_specs=pl.BlockSpec(memory_space=pltpu.VMEM),
        scratch_shapes=[
            pltpu.SemaphoreType.DMA,
            pltpu.SemaphoreType.DMA((groups,)),
            pltpu.SemaphoreType.DMA((groups,)),
        ],
        compiler_params=pltpu.CompilerParams(
            collective_id=0, has_side_effects=True, vmem_limit_bytes=16 * 2**20
        ),
    )(own)


def product(a, b, dims=((1,), (0,))):
    return lax.dot_general(
        a, b, (dims, ((), ())), precision=lax.Precision.HIGHEST, preferred_element_type=jnp.float32
    )


def product_t(a, b):
    return product(a, b, ((1,), (1,)))


def spread_lane(x, lane):
    return jnp.broadcast_to(x[:, lane : lane + 1], x.shape)


def spread_row(x, row):
    return jnp.broadcast_to(x[row : row + 1, :], x.shape)


def inverse_low_base(block):
    size = block.shape[0]
    tiles = [block[8 * g : 8 * g + 8, :] for g in range(size // 8)]
    lane = lax.broadcasted_iota(jnp.int32, (8, size), 1)
    sub = lax.broadcasted_iota(jnp.int32, (8, size), 0)
    for g in range(size // 8):
        base = 8 * g
        inside = (lane >= base) & (lane < base + 8)
        later = range(g + 1, size // 8)
        cols = {h: [spread_lane(tiles[h], base + t) for t in range(8)] for h in [g, *later]}
        rows = jnp.where(inside, jnp.where(lane == base + sub, 1.0, 0.0), tiles[g])
        for h in later:
            tiles[h] = jnp.where(inside, 0.0, tiles[h])
        scale = jnp.zeros((8, size), jnp.float32)
        for t in range(8):
            pivots = [spread_row(cols[g][k], t) for k in range(t, 8)]
            row = spread_row(rows, t)
            inv = 1.0 / pivots[0]
            scale = jnp.where(sub == t, lax.rsqrt(pivots[0]), scale)
            factor = jnp.where(sub > t, cols[g][t] * inv, 0.0)
            rows = rows - factor * row
            for k in range(t + 1, 8):
                cols[g][k] = cols[g][k] - factor * pivots[k - t]
            for h in later:
                factor = cols[h][t] * inv
                tiles[h] = tiles[h] - factor * row
                for k in range(t + 1, 8):
                    cols[h][k] = cols[h][k] - factor * pivots[k - t]
        tiles[g] = jnp.where(lane < base + 8, rows, 0.0) * scale
    return jnp.concatenate(tiles, axis=0)


def inverse_low(block):
    size = block.shape[0]
    if size <= 128:
        return inverse_low_base(block)
    half = size // 2
    first = inverse_low(block[:half, :half])
    below = product_t(block[half:, :half], first)
    second = inverse_low(block[half:, half:] - product_t(below, below))
    corner = -product(second, product(below, first))
    top = jnp.concatenate([first, jnp.zeros_like(first)], axis=1)
    return jnp.concatenate([top, jnp.concatenate([corner, second], axis=1)], axis=0)


def symmetric(block):
    return 0.5 * (block + block.T)


def factor_kernel(strips, slab_ref, out_ref, solve_rows, solve_cols):
    strip = DONE // strips
    low0 = inverse_low(symmetric(slab_ref[:PB, :PB]))
    upper = product(low0, slab_ref[:PB, PB:DONE])
    column = product_t(slab_ref[PB:DONE, :PB], low0)
    low1 = inverse_low(symmetric(slab_ref[PB:DONE, PB:DONE] - product(column, upper)))
    zero = jnp.zeros((PB, PB), jnp.float32)
    by_strip = []
    for ref, cross in ((solve_rows, upper.T), (solve_cols, column)):
        below = jnp.concatenate([-product(low1, product(cross, low0)), low1], axis=1)
        solve = jnp.concatenate([jnp.concatenate([low0, zero], axis=1), below], axis=0)
        for c in range(DONE // 128):
            ref[c] = solve[:, c * 128 : (c + 1) * 128]
        chunks = []
        for c in range(DONE // 128):
            picked = [ref[c, pl.ds(s, strip, stride=strips), :] for s in range(strips)]
            chunks.append(jnp.concatenate(picked, axis=0))
        by_strip.append(jnp.concatenate(chunks, axis=1))
    upper_all = product(by_strip[1], slab_ref[:DONE, DONE:])
    columns = product_t(slab_ref[DONE:, :DONE], by_strip[0])
    trailing = slab_ref[DONE:, DONE:] - product(columns, upper_all)
    for s in range(strips):
        cut = slice(s * strip, (s + 1) * strip)
        out_ref[s, :, :strip] = columns[:, cut].astype(out_ref.dtype)
        out_ref[s, :, strip:] = trailing[:, cut].astype(out_ref.dtype)


def factor(slab, strips):
    row_count = slab.shape[0] - DONE
    return pl.pallas_call(
        functools.partial(factor_kernel, strips),
        out_shape=jax.ShapeDtypeStruct((strips, row_count, P_SIZE // strips), jnp.bfloat16),
        in_specs=[pl.BlockSpec(memory_space=pltpu.VMEM)],
        out_specs=pl.BlockSpec(memory_space=pltpu.VMEM),
        scratch_shapes=[pltpu.VMEM((DONE // 128, DONE, 128), jnp.float32)] * 2,
        compiler_params=pltpu.CompilerParams(vmem_limit_bytes=48 * 2**20),
    )(slab)


def local(constraint_rows, metric):
    n_wide, strips = lax.axis_size("wide"), lax.axis_size("narrow")
    groups = n_wide * strips
    depth = P_SIZE // groups
    order = metric.shape[0]
    own_rows = constraint_rows[:, 0, :]
    gathered = gather_panel(own_rows[:depth], n_wide, strips)
    gathered = gathered.reshape(n_wide, strips, depth, order)
    ahead = DONE // groups
    first = gathered[:, :, :ahead].transpose(2, 0, 1, 3).reshape(DONE, order)
    rest = gathered[:, :, ahead:].transpose(1, 2, 0, 3).reshape(P_SIZE - DONE, order)
    panel = jnp.concatenate([first, rest], axis=0)
    rows = jnp.concatenate([first, own_rows], axis=0)
    projected = jnp.dot(rows, metric, preferred_element_type=jnp.float32).astype(jnp.bfloat16)
    gram = lax.dot_general(
        projected, panel, (((1,), (1,)), ((), ())), preferred_element_type=jnp.float32
    )
    strips_out = factor(gram * gram, strips)
    mine = lax.all_to_all(strips_out, "narrow", split_axis=0, concat_axis=0, tiled=True)
    return mine.astype(jnp.float32).transpose(1, 0, 2)[:, :, None, :]


def solution(mesh):
    placed = (P(None, ("wide", "narrow"), None), P())
    return jax.shard_map(
        local,
        mesh=mesh,
        in_specs=placed,
        out_specs=P(None, "wide", "narrow", None),
        check_vma=False,
    )
```

```python
import functools

import jax
import jax.numpy as jnp
from jax import lax
from jax.experimental import pallas as pl
from jax.experimental.pallas import tpu as pltpu
from jax.sharding import PartitionSpec as P

P_SIZE = 1024
PB = 256
NPANEL = 2
DONE = PB * NPANEL
MESH = pl.DeviceIdType.MESH


def gather_kernel(n_wide, n_narrow, first_ref, rest_ref, firsts_ref, rests_ref, own_sem, send_sem, recv_sem):
    w, z = lax.axis_index("wide"), lax.axis_index("narrow")
    groups = n_wide * n_narrow
    mates = [lax.rem(w + 2 * i, n_wide) for i in range(1, n_wide // 2)]
    twin = w + 1 - 2 * lax.rem(w, 2)
    column = [lax.rem(z + i, n_narrow) for i in range(1, n_narrow)]

    barrier = pltpu.get_barrier_semaphore()
    partners = [(w, p) for p in column] + [(m, z) for m in mates] + [(twin, z)]
    for partner in partners:
        pl.semaphore_signal(barrier, inc=1, device_id=partner, device_id_type=MESH)
    pl.semaphore_wait(barrier, len(partners))

    sent = []

    def send(src, dst, sem, target):
        copy = pltpu.make_async_remote_copy(
            src_ref=src,
            dst_ref=dst,
            send_sem=send_sem.at[len(sent)],
            recv_sem=recv_sem.at[sem],
            device_id=target,
            device_id_type=MESH,
        )
        copy.start()
        sent.append(copy)

    def arrived(ref, sem):
        pltpu.make_async_remote_copy(
            src_ref=first_ref,
            dst_ref=ref,
            send_sem=send_sem.at[0],
            recv_sem=recv_sem.at[sem],
            device_id=(twin, z),
            device_id_type=MESH,
        ).wait_recv()

    me = w * n_narrow + z
    for p in column:
        send(first_ref, firsts_ref.at[me], me, (w, p))
    for m in mates:
        send(first_ref, firsts_ref.at[me], me, (m, z))
    send(first_ref, firsts_ref.at[me], me, (twin, z))
    keep = [
        pltpu.make_async_copy(first_ref, firsts_ref.at[me], own_sem.at[0]),
        pltpu.make_async_copy(rest_ref, rests_ref.at[w], own_sem.at[1]),
    ]
    for copy in keep:
        copy.start()
    for p in column:
        slot = w * n_narrow + p
        arrived(firsts_ref.at[slot], slot)
        for m in mates:
            send(firsts_ref.at[slot], firsts_ref.at[slot], slot, (m, z))
        send(firsts_ref.at[slot], firsts_ref.at[slot], slot, (twin, z))
    for m in mates + [twin]:
        send(rest_ref, rests_ref.at[w], groups + w, (m, z))
    for p in [z] + column:
        for m in mates:
            slot = m * n_narrow + p
            arrived(firsts_ref.at[slot], slot)
            send(firsts_ref.at[slot], firsts_ref.at[slot], slot, (twin, z))
    for m in mates:
        arrived(rests_ref.at[m], groups + m)
        send(rests_ref.at[m], rests_ref.at[m], groups + m, (twin, z))
    for m in [w] + mates:
        other = m + 1 - 2 * lax.rem(m, 2)
        for p in [z] + column:
            slot = other * n_narrow + p
            arrived(firsts_ref.at[slot], slot)
        arrived(rests_ref.at[other], groups + other)
    for copy in keep:
        copy.wait()
    for copy in sent:
        copy.wait_send()


def gather_panel(first, rest, n_wide, n_narrow):
    groups = n_wide * n_narrow
    in_vmem = pl.BlockSpec(memory_space=pltpu.VMEM)
    return pl.pallas_call(
        functools.partial(gather_kernel, n_wide, n_narrow),
        out_shape=[
            jax.ShapeDtypeStruct((groups,) + first.shape, first.dtype),
            jax.ShapeDtypeStruct((n_wide,) + rest.shape, rest.dtype),
        ],
        in_specs=[in_vmem] * 2,
        out_specs=[in_vmem] * 2,
        scratch_shapes=[
            pltpu.SemaphoreType.DMA((2,)),
            pltpu.SemaphoreType.DMA((groups + n_wide,)),
            pltpu.SemaphoreType.DMA((groups + n_wide,)),
        ],
        compiler_params=pltpu.CompilerParams(
            collective_id=0, has_side_effects=True, vmem_limit_bytes=16 * 2**20
        ),
    )(first, rest)


def product(a, b, dims=((1,), (0,))):
    return lax.dot_general(
        a, b, (dims, ((), ())), precision=lax.Precision.HIGHEST, preferred_element_type=jnp.float32
    )


def product_t(a, b):
    return product(a, b, ((1,), (1,)))


def spread_lane(x, lane):
    return jnp.broadcast_to(x[:, lane : lane + 1], x.shape)


def inverse_low_base(block):
    size = block.shape[0]
    rest = block
    done = []
    for g in range(size // 8):
        base = 8 * g
        lane = lax.broadcasted_iota(jnp.int32, (8, size), 1)
        sub = lax.broadcasted_iota(jnp.int32, (8, size), 0)
        rows, rest = rest[:8], rest[8:]
        last = g == size // 8 - 1
        cols = [spread_lane(rows, base + t) for t in range(8)]
        inside = (lane >= base) & (lane < base + 8)
        rows = jnp.where(inside, jnp.where(lane == base + sub, 1.0, 0.0), rows)
        if not last:
            below = [spread_lane(rest, base + t) for t in range(8)]
            lanes = lax.broadcasted_iota(jnp.int32, rest.shape, 1)
            rest = jnp.where((lanes >= base) & (lanes < base + 8), 0.0, rest)
        scale = jnp.zeros((8, size), jnp.float32)
        for t in range(8):
            pivots = [cols[k][t : t + 1, :] for k in range(t, 8)]
            row = rows[t : t + 1, :]
            inv = 1.0 / pivots[0]
            scale = jnp.where(sub == t, lax.rsqrt(pivots[0]), scale)
            factor = jnp.where(sub > t, cols[t] * inv, 0.0)
            rows = rows - factor * row
            for k in range(t + 1, 8):
                cols[k] = cols[k] - factor * pivots[k - t]
            if not last:
                factor = below[t] * inv
                rest = rest - factor * row
                for k in range(t + 1, 8):
                    below[k] = below[k] - factor * pivots[k - t]
        done.append(jnp.where(lane < base + 8, rows, 0.0) * scale)
    return jnp.concatenate(done, axis=0)


def inverse_low(block):
    size = block.shape[0]
    if size <= 128:
        return inverse_low_base(block)
    half = size // 2
    first = inverse_low(block[:half, :half])
    below = product_t(block[half:, :half], first)
    second = inverse_low(block[half:, half:] - product_t(below, below))
    corner = -product(second, product(below, first))
    top = jnp.concatenate([first, jnp.zeros_like(first)], axis=1)
    return jnp.concatenate([top, jnp.concatenate([corner, second], axis=1)], axis=0)


def symmetric(block):
    return 0.5 * (block + block.T)


def bf16_product_t(a, b):
    return lax.dot_general(a, b, (((1,), (1,)), ((), ())), preferred_element_type=jnp.float32)


def two_terms(x):
    high = x.astype(jnp.bfloat16)
    return high, (x - high.astype(jnp.float32)).astype(jnp.bfloat16)


def factor_kernel(strips, panel_ref, metric_ref, weight_ref, high_ref, low_ref, solve_rows):
    strip = DONE // strips
    own = lax.axis_index("narrow")
    weighted = jnp.dot(panel_ref[...], metric_ref[...], preferred_element_type=jnp.float32)
    high, low = two_terms(weighted)
    high_ref[...], low_ref[...] = high, low
    gram = bf16_product_t(panel_ref[:DONE], high) + bf16_product_t(panel_ref[:DONE], low)
    slab = gram * gram

    low0 = inverse_low(symmetric(slab[:PB, :PB]))
    upper = product(low0, slab[:PB, PB:DONE])
    column = product_t(slab[PB:DONE, :PB], low0)
    low1 = inverse_low(symmetric(slab[PB:DONE, PB:DONE] - product(column, upper)))
    zero = jnp.zeros((PB, PB), jnp.float32)
    solves = []
    for cross in (upper.T, column):
        below = jnp.concatenate([-product(low1, product(cross, low0)), low1], axis=1)
        solves.append(jnp.concatenate([jnp.concatenate([low0, zero], axis=1), below], axis=0))
    chunks = []
    for c in range(DONE // 128):
        solve_rows[c] = solves[0][:, c * 128 : (c + 1) * 128]
        picked = solve_rows[c, pl.ds(0, strip, stride=strips), :]
        for s in range(1, strips):
            picked = jnp.where(own == s, solve_rows[c, pl.ds(s, strip, stride=strips), :], picked)
        chunks.append(picked)
    weight_ref[:, :strip] = jnp.concatenate(chunks, axis=1).T
    weight_ref[:, strip:] = product(solves[0], product(solves[1], slab[:, DONE:]), ((0,), (0,)))


def factor(panel, metric, strips):
    in_vmem = pl.BlockSpec(memory_space=pltpu.VMEM)
    terms = jax.ShapeDtypeStruct(panel.shape, jnp.bfloat16)
    width = P_SIZE // strips
    flops = 2 * panel.shape[0] * panel.shape[1] * metric.shape[0] * 20
    return pl.pallas_call(
        functools.partial(factor_kernel, strips),
        out_shape=[jax.ShapeDtypeStruct((DONE, width), jnp.float32), terms, terms],
        in_specs=[in_vmem] * 2,
        out_specs=[in_vmem] * 3,
        scratch_shapes=[pltpu.VMEM((DONE // 128, DONE, 128), jnp.float32)],
        compiler_params=pltpu.CompilerParams(vmem_limit_bytes=48 * 2**20),
        cost_estimate=pl.CostEstimate(flops=flops, bytes_accessed=2**22, transcendentals=0),
    )(panel, metric)


def finish_kernel(rows_ref, high_ref, low_ref, weight_ref, out_ref):
    strips, row_count, order = rows_ref.shape
    strip = DONE // strips
    rows = rows_ref[...].reshape(strips * row_count, order)
    gram = bf16_product_t(rows, high_ref[...]) + bf16_product_t(rows, low_ref[...])
    slab = gram * gram
    solved = product(slab[:, :DONE], weight_ref[...])
    for s in range(strips):
        part = slice(s * row_count, (s + 1) * row_count)
        trailing = slab[part, DONE:] - solved[part, strip:]
        out_ref[:, s] = jnp.concatenate([solved[part, :strip], trailing], axis=1)[:, None, :]


def finish(rows, high, low, weight):
    strips, row_count, order = rows.shape
    width = weight.shape[1]
    block = 128
    whole = lambda x: pl.BlockSpec(x.shape, lambda i: (0, 0))
    return pl.pallas_call(
        finish_kernel,
        out_shape=jax.ShapeDtypeStruct((row_count, strips, 1, width), jnp.float32),
        grid=(row_count // block,),
        in_specs=[
            pl.BlockSpec((strips, block, order), lambda i: (0, i, 0)),
            whole(high),
            whole(low),
            whole(weight),
        ],
        out_specs=pl.BlockSpec((block, strips, 1, width), lambda i: (i, 0, 0, 0)),
        compiler_params=pltpu.CompilerParams(vmem_limit_bytes=48 * 2**20),
    )(rows, high, low, weight)


def local(constraint_rows, metric):
    n_wide, strips = lax.axis_size("wide"), lax.axis_size("narrow")
    groups = n_wide * strips
    depth = P_SIZE // groups
    ahead = DONE // groups
    order = metric.shape[0]
    own_rows = constraint_rows[:, 0, :]
    rows = lax.all_gather(own_rows, "narrow", axis=0, tiled=False)
    firsts, rests = gather_panel(own_rows[:ahead], own_rows[ahead:depth], n_wide, strips)
    first = firsts.transpose(1, 0, 2).reshape(DONE, order)
    rest = rests.transpose(1, 0, 2).reshape((P_SIZE - DONE) // strips, order)
    weight, high, low = factor(jnp.concatenate([first, rest], axis=0), metric, strips)
    return finish(rows, high, low, weight)


def solution(mesh):
    placed = (P(None, ("wide", "narrow"), None), P())
    return jax.shard_map(
        local,
        mesh=mesh,
        in_specs=placed,
        out_specs=P(None, "wide", "narrow", None),
        check_vma=False,
    )
```

```python
import functools

import jax
import jax.numpy as jnp
from jax import lax
from jax.experimental import pallas as pl
from jax.experimental.pallas import tpu as pltpu
from jax.sharding import PartitionSpec as P

P_SIZE = 1024
PB = 256
NPANEL = 2
DONE = PB * NPANEL
MESH = pl.DeviceIdType.MESH


def gather_kernel(n_wide, n_narrow, own_ref, out_ref, own_sem, send_sem, recv_sem):
    w, z = lax.axis_index("wide"), lax.axis_index("narrow")
    mates = [lax.rem(w + 2 * i, n_wide) for i in range(1, n_wide // 2)]
    twin = w + 1 - 2 * lax.rem(w, 2)
    column = [lax.rem(z + i, n_narrow) for i in range(1, n_narrow)]

    barrier = pltpu.get_barrier_semaphore()
    partners = [(w, p) for p in column] + [(m, z) for m in mates] + [(twin, z)]
    for partner in partners:
        pl.semaphore_signal(barrier, inc=1, device_id=partner, device_id_type=MESH)
    pl.semaphore_wait(barrier, len(partners))

    sent = []

    def send(src, slot, target):
        copy = pltpu.make_async_remote_copy(
            src_ref=src,
            dst_ref=out_ref.at[slot],
            send_sem=send_sem.at[len(sent)],
            recv_sem=recv_sem.at[slot],
            device_id=target,
            device_id_type=MESH,
        )
        copy.start()
        sent.append(copy)

    def arrived(slot):
        pltpu.make_async_remote_copy(
            src_ref=own_ref,
            dst_ref=out_ref.at[slot],
            send_sem=send_sem.at[0],
            recv_sem=recv_sem.at[slot],
            device_id=(twin, z),
            device_id_type=MESH,
        ).wait_recv()

    me = w * n_narrow + z
    for p in column:
        send(own_ref, me, (w, p))
    for m in mates:
        send(own_ref, me, (m, z))
    send(own_ref, me, (twin, z))
    keep = pltpu.make_async_copy(own_ref, out_ref.at[me], own_sem)
    keep.start()
    for p in column:
        slot = w * n_narrow + p
        arrived(slot)
        for m in mates:
            send(out_ref.at[slot], slot, (m, z))
        send(out_ref.at[slot], slot, (twin, z))
    for p in [z] + column:
        for m in mates:
            slot = m * n_narrow + p
            arrived(slot)
            send(out_ref.at[slot], slot, (twin, z))
    for p in [z] + column:
        for m in [w] + mates:
            arrived((m + 1 - 2 * lax.rem(m, 2)) * n_narrow + p)
    keep.wait()
    for copy in sent:
        copy.wait_send()


def gather_panel(own, n_wide, n_narrow):
    groups = n_wide * n_narrow
    return pl.pallas_call(
        functools.partial(gather_kernel, n_wide, n_narrow),
        out_shape=jax.ShapeDtypeStruct((groups,) + own.shape, own.dtype),
        in_specs=[pl.BlockSpec(memory_space=pltpu.VMEM)],
        out_specs=pl.BlockSpec(memory_space=pltpu.VMEM),
        scratch_shapes=[
            pltpu.SemaphoreType.DMA,
            pltpu.SemaphoreType.DMA((groups,)),
            pltpu.SemaphoreType.DMA((groups,)),
        ],
        compiler_params=pltpu.CompilerParams(
            collective_id=0, has_side_effects=True, vmem_limit_bytes=16 * 2**20
        ),
    )(own)


def product(a, b, dims=((1,), (0,))):
    return lax.dot_general(
        a, b, (dims, ((), ())), precision=lax.Precision.HIGHEST, preferred_element_type=jnp.float32
    )


def product_t(a, b):
    return product(a, b, ((1,), (1,)))


def spread_lane(x, lane):
    return jnp.broadcast_to(x[:, lane : lane + 1], x.shape)


def inverse_low_base(block):
    size = block.shape[0]
    rest = block
    done = []
    for g in range(size // 8):
        base = 8 * g
        lane = lax.broadcasted_iota(jnp.int32, (8, size), 1)
        sub = lax.broadcasted_iota(jnp.int32, (8, size), 0)
        rows, rest = rest[:8], rest[8:]
        last = g == size // 8 - 1
        cols = [spread_lane(rows, base + t) for t in range(8)]
        inside = (lane >= base) & (lane < base + 8)
        rows = jnp.where(inside, jnp.where(lane == base + sub, 1.0, 0.0), rows)
        if not last:
            below = [spread_lane(rest, base + t) for t in range(8)]
            lanes = lax.broadcasted_iota(jnp.int32, rest.shape, 1)
            rest = jnp.where((lanes >= base) & (lanes < base + 8), 0.0, rest)
        scale = jnp.zeros((8, size), jnp.float32)
        for t in range(8):
            pivots = [cols[k][t : t + 1, :] for k in range(t, 8)]
            row = rows[t : t + 1, :]
            inv = 1.0 / pivots[0]
            scale = jnp.where(sub == t, lax.rsqrt(pivots[0]), scale)
            factor = jnp.where(sub > t, cols[t] * inv, 0.0)
            rows = rows - factor * row
            for k in range(t + 1, 8):
                cols[k] = cols[k] - factor * pivots[k - t]
            if not last:
                factor = below[t] * inv
                rest = rest - factor * row
                for k in range(t + 1, 8):
                    below[k] = below[k] - factor * pivots[k - t]
        done.append(jnp.where(lane < base + 8, rows, 0.0) * scale)
    return jnp.concatenate(done, axis=0)


def inverse_low(block):
    size = block.shape[0]
    if size <= 128:
        return inverse_low_base(block)
    half = size // 2
    first = inverse_low(block[:half, :half])
    below = product_t(block[half:, :half], first)
    second = inverse_low(block[half:, half:] - product_t(below, below))
    corner = -product(second, product(below, first))
    top = jnp.concatenate([first, jnp.zeros_like(first)], axis=1)
    return jnp.concatenate([top, jnp.concatenate([corner, second], axis=1)], axis=0)


def symmetric(block):
    return 0.5 * (block + block.T)


def bf16_product_t(a, b):
    return lax.dot_general(a, b, (((1,), (1,)), ((), ())), preferred_element_type=jnp.float32)


def two_terms(x):
    high = x.astype(jnp.bfloat16)
    return high, (x - high.astype(jnp.float32)).astype(jnp.bfloat16)


def factor_kernel(strips, panel_ref, metric_ref, solve_ref, upper_ref, high_ref, low_ref, chunk_ref):
    strip = DONE // strips
    weighted = jnp.dot(panel_ref[...], metric_ref[...], preferred_element_type=jnp.float32)
    high, low = two_terms(weighted)
    high_ref[...], low_ref[...] = high, low
    gram = bf16_product_t(panel_ref[:DONE], high) + bf16_product_t(panel_ref[:DONE], low)
    slab = gram * gram

    low0 = inverse_low(symmetric(slab[:PB, :PB]))
    upper = product(low0, slab[:PB, PB:DONE])
    column = product_t(slab[PB:DONE, :PB], low0)
    low1 = inverse_low(symmetric(slab[PB:DONE, PB:DONE] - product(column, upper)))
    zero = jnp.zeros((PB, PB), jnp.float32)
    by_strip = []
    for which, cross in enumerate((upper.T, column)):
        below = jnp.concatenate([-product(low1, product(cross, low0)), low1], axis=1)
        solve = jnp.concatenate([jnp.concatenate([low0, zero], axis=1), below], axis=0)
        chunks = []
        for c in range(DONE // 128):
            chunk_ref[which, c] = solve[:, c * 128 : (c + 1) * 128]
            picked = [chunk_ref[which, c, pl.ds(s, strip, stride=strips), :] for s in range(strips)]
            chunks.append(jnp.concatenate(picked, axis=0))
        by_strip.append(jnp.concatenate(chunks, axis=1))
    solve_ref[...] = by_strip[0]
    upper_ref[...] = product(by_strip[1], slab[:, DONE:])


def factor(panel, metric, strips):
    in_vmem = pl.BlockSpec(memory_space=pltpu.VMEM)
    terms = jax.ShapeDtypeStruct(panel.shape, jnp.bfloat16)
    return pl.pallas_call(
        functools.partial(factor_kernel, strips),
        out_shape=[
            jax.ShapeDtypeStruct((DONE, DONE), jnp.float32),
            jax.ShapeDtypeStruct((DONE, P_SIZE - DONE), jnp.float32),
            terms,
            terms,
        ],
        in_specs=[in_vmem] * 2,
        out_specs=[in_vmem] * 4,
        scratch_shapes=[pltpu.VMEM((2, DONE // 128, DONE, 128), jnp.float32)],
        compiler_params=pltpu.CompilerParams(vmem_limit_bytes=48 * 2**20),
    )(panel, metric)


def finish_kernel(
    strips, chunks, rows_ref, high_ref, low_ref, solve_ref, upper_ref, out_ref, made, own_sem, send_sem, recv_sem
):
    w, z = lax.axis_index("wide"), lax.axis_index("narrow")
    column = [lax.rem(z + i, strips) for i in range(1, strips)]
    strip = DONE // strips
    block = rows_ref.shape[0] // chunks
    barrier = pltpu.get_barrier_semaphore()
    for p in column:
        pl.semaphore_signal(barrier, inc=1, device_id=(w, p), device_id_type=MESH)

    copies, kept = [], []
    for c in range(chunks):
        part = pl.ds(c * block, block)
        rows = rows_ref[part, :]
        gram = bf16_product_t(rows, high_ref[...]) + bf16_product_t(rows, low_ref[...])
        slab = gram * gram
        solved = product_t(slab[:, :DONE], solve_ref[...])
        trailing = slab[:, DONE:] - product(solved, upper_ref[...])
        for s in range(strips):
            cut = slice(s * strip, (s + 1) * strip)
            both = jnp.concatenate([solved[:, cut], trailing[:, cut]], axis=1)
            made[s, part, :] = both.astype(made.dtype)
        if c == 0:
            pl.semaphore_wait(barrier, strips - 1)
        for i, p in enumerate(column):
            copy = pltpu.make_async_remote_copy(
                src_ref=made.at[p, part],
                dst_ref=out_ref.at[z, part],
                send_sem=send_sem.at[c, i],
                recv_sem=recv_sem.at[c, z],
                device_id=(w, p),
                device_id_type=MESH,
            )
            copy.start()
            copies.append(copy)
        keep = pltpu.make_async_copy(made.at[z, part], out_ref.at[z, part], own_sem.at[c])
        keep.start()
        kept.append(keep)
    for c in range(chunks):
        part = pl.ds(c * block, block)
        for p in column:
            pltpu.make_async_remote_copy(
                src_ref=made.at[p, part],
                dst_ref=out_ref.at[p, part],
                send_sem=send_sem.at[c, 0],
                recv_sem=recv_sem.at[c, p],
                device_id=(w, p),
                device_id_type=MESH,
            ).wait_recv()
        kept[c].wait()
    for copy in copies:
        copy.wait_send()


def finish(rows, high, low, solve, upper, strips):
    row_count = rows.shape[0]
    chunks = 4
    in_vmem = pl.BlockSpec(memory_space=pltpu.VMEM)
    out = jax.ShapeDtypeStruct((strips, row_count, P_SIZE // strips), jnp.bfloat16)
    return pl.pallas_call(
        functools.partial(finish_kernel, strips, chunks),
        out_shape=out,
        in_specs=[in_vmem] * 5,
        out_specs=in_vmem,
        scratch_shapes=[
            pltpu.VMEM(out.shape, out.dtype),
            pltpu.SemaphoreType.DMA((chunks,)),
            pltpu.SemaphoreType.DMA((chunks, strips - 1)),
            pltpu.SemaphoreType.DMA((chunks, strips)),
        ],
        compiler_params=pltpu.CompilerParams(
            collective_id=1, has_side_effects=True, vmem_limit_bytes=48 * 2**20
        ),
    )(rows, high, low, solve, upper)


def local(constraint_rows, metric):
    n_wide, strips = lax.axis_size("wide"), lax.axis_size("narrow")
    groups = n_wide * strips
    depth = P_SIZE // groups
    ahead = DONE // groups
    order = metric.shape[0]
    own_rows = constraint_rows[:, 0, :]
    gathered = gather_panel(own_rows[:depth], n_wide, strips)
    gathered = gathered.reshape(n_wide, strips, depth, order)
    first = gathered[:, :, :ahead].transpose(2, 0, 1, 3).reshape(DONE, order)
    rest = gathered[:, :, ahead:].transpose(1, 2, 0, 3).reshape(P_SIZE - DONE, order)
    panel = jnp.concatenate([first, rest], axis=0)
    solve, upper, high, low = factor(panel, metric, strips)
    mine = finish(own_rows, high, low, solve, upper, strips)
    return mine.astype(jnp.float32).transpose(1, 0, 2)[:, :, None, :]


def solution(mesh):
    placed = (P(None, ("wide", "narrow"), None), P())
    return jax.shard_map(
        local,
        mesh=mesh,
        in_specs=placed,
        out_specs=P(None, "wide", "narrow", None),
        check_vma=False,
    )
```

```python
import functools

import jax
import jax.numpy as jnp
from jax import lax
from jax.experimental import pallas as pl
from jax.experimental.pallas import tpu as pltpu
from jax.sharding import PartitionSpec as P

P_SIZE = 1024
PB = 256
NPANEL = 2
DONE = PB * NPANEL
MESH = pl.DeviceIdType.MESH


def gather_kernel(n_wide, n_narrow, own_ref, out_ref, own_sem, send_sem, recv_sem):
    w, z = lax.axis_index("wide"), lax.axis_index("narrow")
    mates = [lax.rem(w + 2 * i, n_wide) for i in range(1, n_wide // 2)]
    twin = w + 1 - 2 * lax.rem(w, 2)
    column = [lax.rem(z + i, n_narrow) for i in range(1, n_narrow)]

    barrier = pltpu.get_barrier_semaphore()
    partners = [(w, p) for p in column] + [(m, z) for m in mates] + [(twin, z)]
    for partner in partners:
        pl.semaphore_signal(barrier, inc=1, device_id=partner, device_id_type=MESH)
    pl.semaphore_wait(barrier, len(partners))

    sent = []

    def send(src, slot, target):
        copy = pltpu.make_async_remote_copy(
            src_ref=src,
            dst_ref=out_ref.at[slot],
            send_sem=send_sem.at[len(sent)],
            recv_sem=recv_sem.at[slot],
            device_id=target,
            device_id_type=MESH,
        )
        copy.start()
        sent.append(copy)

    def arrived(slot):
        pltpu.make_async_remote_copy(
            src_ref=own_ref,
            dst_ref=out_ref.at[slot],
            send_sem=send_sem.at[0],
            recv_sem=recv_sem.at[slot],
            device_id=(twin, z),
            device_id_type=MESH,
        ).wait_recv()

    me = w * n_narrow + z
    for p in column:
        send(own_ref, me, (w, p))
    for m in mates:
        send(own_ref, me, (m, z))
    send(own_ref, me, (twin, z))
    keep = pltpu.make_async_copy(own_ref, out_ref.at[me], own_sem)
    keep.start()
    for p in column:
        slot = w * n_narrow + p
        arrived(slot)
        for m in mates:
            send(out_ref.at[slot], slot, (m, z))
        send(out_ref.at[slot], slot, (twin, z))
    for p in [z] + column:
        for m in mates:
            slot = m * n_narrow + p
            arrived(slot)
            send(out_ref.at[slot], slot, (twin, z))
    for p in [z] + column:
        for m in [w] + mates:
            arrived((m + 1 - 2 * lax.rem(m, 2)) * n_narrow + p)
    keep.wait()
    for copy in sent:
        copy.wait_send()


def gather_panel(own, n_wide, n_narrow):
    groups = n_wide * n_narrow
    return pl.pallas_call(
        functools.partial(gather_kernel, n_wide, n_narrow),
        out_shape=jax.ShapeDtypeStruct((groups,) + own.shape, own.dtype),
        in_specs=[pl.BlockSpec(memory_space=pltpu.VMEM)],
        out_specs=pl.BlockSpec(memory_space=pltpu.VMEM),
        scratch_shapes=[
            pltpu.SemaphoreType.DMA,
            pltpu.SemaphoreType.DMA((groups,)),
            pltpu.SemaphoreType.DMA((groups,)),
        ],
        compiler_params=pltpu.CompilerParams(
            collective_id=0, has_side_effects=True, vmem_limit_bytes=16 * 2**20
        ),
    )(own)


def product(a, b, dims=((1,), (0,))):
    return lax.dot_general(
        a, b, (dims, ((), ())), precision=lax.Precision.HIGHEST, preferred_element_type=jnp.float32
    )


def product_t(a, b):
    return product(a, b, ((1,), (1,)))


def spread_lane(x, lane):
    return jnp.broadcast_to(x[:, lane : lane + 1], x.shape)


def inverse_low_base(block):
    size = block.shape[0]
    rest = block
    done = []
    for g in range(size // 8):
        base = 8 * g
        lane = lax.broadcasted_iota(jnp.int32, (8, size), 1)
        sub = lax.broadcasted_iota(jnp.int32, (8, size), 0)
        rows, rest = rest[:8], rest[8:]
        last = g == size // 8 - 1
        cols = [spread_lane(rows, base + t) for t in range(8)]
        inside = (lane >= base) & (lane < base + 8)
        rows = jnp.where(inside, jnp.where(lane == base + sub, 1.0, 0.0), rows)
        if not last:
            below = [spread_lane(rest, base + t) for t in range(8)]
            lanes = lax.broadcasted_iota(jnp.int32, rest.shape, 1)
            rest = jnp.where((lanes >= base) & (lanes < base + 8), 0.0, rest)
        scale = jnp.zeros((8, size), jnp.float32)
        for t in range(8):
            pivots = [cols[k][t : t + 1, :] for k in range(t, 8)]
            row = rows[t : t + 1, :]
            inv = 1.0 / pivots[0]
            scale = jnp.where(sub == t, lax.rsqrt(pivots[0]), scale)
            factor = jnp.where(sub > t, cols[t] * inv, 0.0)
            rows = rows - factor * row
            for k in range(t + 1, 8):
                cols[k] = cols[k] - factor * pivots[k - t]
            if not last:
                factor = below[t] * inv
                rest = rest - factor * row
                for k in range(t + 1, 8):
                    below[k] = below[k] - factor * pivots[k - t]
        done.append(jnp.where(lane < base + 8, rows, 0.0) * scale)
    return jnp.concatenate(done, axis=0)


def inverse_low(block):
    size = block.shape[0]
    if size <= 128:
        return inverse_low_base(block)
    half = size // 2
    first = inverse_low(block[:half, :half])
    below = product_t(block[half:, :half], first)
    second = inverse_low(block[half:, half:] - product_t(below, below))
    corner = -product(second, product(below, first))
    top = jnp.concatenate([first, jnp.zeros_like(first)], axis=1)
    return jnp.concatenate([top, jnp.concatenate([corner, second], axis=1)], axis=0)


def symmetric(block):
    return 0.5 * (block + block.T)


def bf16_product_t(a, b):
    return lax.dot_general(a, b, (((1,), (1,)), ((), ())), preferred_element_type=jnp.float32)


def two_terms(x):
    high = x.astype(jnp.bfloat16)
    return high, (x - high.astype(jnp.float32)).astype(jnp.bfloat16)


def factor_kernel(strips, panel_ref, metric_ref, solve_ref, upper_ref, weight_ref, high_ref, low_ref, chunk_ref):
    strip = DONE // strips
    weighted = jnp.dot(panel_ref[...], metric_ref[...], preferred_element_type=jnp.float32)
    high, low = two_terms(weighted)
    high_ref[...], low_ref[...] = high, low
    gram = bf16_product_t(panel_ref[:DONE], high) + bf16_product_t(panel_ref[:DONE], low)
    slab = gram * gram

    low0 = inverse_low(symmetric(slab[:PB, :PB]))
    upper = product(low0, slab[:PB, PB:DONE])
    column = product_t(slab[PB:DONE, :PB], low0)
    low1 = inverse_low(symmetric(slab[PB:DONE, PB:DONE] - product(column, upper)))
    zero = jnp.zeros((PB, PB), jnp.float32)
    by_strip = []
    for which, cross in enumerate((upper.T, column)):
        below = jnp.concatenate([-product(low1, product(cross, low0)), low1], axis=1)
        solve = jnp.concatenate([jnp.concatenate([low0, zero], axis=1), below], axis=0)
        chunks = []
        for c in range(DONE // 128):
            chunk_ref[which, c] = solve[:, c * 128 : (c + 1) * 128]
            picked = [chunk_ref[which, c, pl.ds(s, strip, stride=strips), :] for s in range(strips)]
            chunks.append(jnp.concatenate(picked, axis=0))
        by_strip.append(jnp.concatenate(chunks, axis=1))
    solve_ref[...] = by_strip[0]
    upper_all = product(by_strip[1], slab[:, DONE:])
    upper_ref[...] = upper_all

    own = lax.axis_index("narrow")
    solve_own, upper_own = by_strip[0][:strip], upper_all[:, :strip]
    for s in range(1, strips):
        cut = slice(s * strip, (s + 1) * strip)
        solve_own = jnp.where(own == s, by_strip[0][cut], solve_own)
        upper_own = jnp.where(own == s, upper_all[:, cut], upper_own)
    weight_ref[:, :strip] = solve_own.T
    weight_ref[:, strip:] = product(by_strip[0], upper_own, ((0,), (0,)))


def factor(panel, metric, strips):
    in_vmem = pl.BlockSpec(memory_space=pltpu.VMEM)
    terms = jax.ShapeDtypeStruct(panel.shape, jnp.bfloat16)
    return pl.pallas_call(
        functools.partial(factor_kernel, strips),
        out_shape=[
            jax.ShapeDtypeStruct((DONE, DONE), jnp.float32),
            jax.ShapeDtypeStruct((DONE, P_SIZE - DONE), jnp.float32),
            jax.ShapeDtypeStruct((DONE, P_SIZE // strips), jnp.float32),
            terms,
            terms,
        ],
        in_specs=[in_vmem] * 2,
        out_specs=[in_vmem] * 5,
        scratch_shapes=[pltpu.VMEM((2, DONE // 128, DONE, 128), jnp.float32)],
        compiler_params=pltpu.CompilerParams(vmem_limit_bytes=48 * 2**20),
    )(panel, metric)


def finish_kernel(
    strips, chunks, rows_ref, near_ref, high_ref, low_ref, solve_ref, upper_ref, weight_ref,
    out_ref, made, near, near_sem, own_sem, send_sem, recv_sem,
):
    w, z = lax.axis_index("wide"), lax.axis_index("narrow")
    column = [lax.rem(z + i, strips) for i in range(1, strips)]
    strip = DONE // strips
    gathered = near_ref.shape[1]
    block = rows_ref.shape[0] // chunks
    fetch = pltpu.make_async_copy(near_ref, near, near_sem)
    fetch.start()
    barrier = pltpu.get_barrier_semaphore()
    for p in column:
        pl.semaphore_signal(barrier, inc=1, device_id=(w, p), device_id_type=MESH)

    copies, kept = [], []
    for c in range(chunks):
        part = pl.ds(gathered + c * block, block)
        rows = rows_ref[pl.ds(c * block, block), :]
        gram = bf16_product_t(rows, high_ref[...]) + bf16_product_t(rows, low_ref[...])
        slab = gram * gram
        solved = product_t(slab[:, :DONE], solve_ref[...])
        trailing = slab[:, DONE:] - product(solved, upper_ref[...])
        for s in range(strips):
            cut = slice(s * strip, (s + 1) * strip)
            both = jnp.concatenate([solved[:, cut], trailing[:, cut]], axis=1)
            made[s, pl.ds(c * block, block), :] = both.astype(made.dtype)
        if c == 0:
            pl.semaphore_wait(barrier, strips - 1)
        for i, p in enumerate(column):
            copy = pltpu.make_async_remote_copy(
                src_ref=made.at[p, pl.ds(c * block, block)],
                dst_ref=out_ref.at[z, part],
                send_sem=send_sem.at[c, i],
                recv_sem=recv_sem.at[c, z],
                device_id=(w, p),
                device_id_type=MESH,
            )
            copy.start()
            copies.append(copy)
        keep = pltpu.make_async_copy(made.at[z, pl.ds(c * block, block)], out_ref.at[z, part], own_sem.at[c])
        keep.start()
        kept.append(keep)

    fetch.wait()
    own_rows = pl.ds(pl.multiple_of(DONE + z * strip, 16), strip)
    for n in range(strips):
        rows = near[n]
        gram = bf16_product_t(rows, high_ref[:DONE]) + bf16_product_t(rows, low_ref[:DONE])
        solved = product(gram * gram, weight_ref[...])
        gram = bf16_product_t(rows, high_ref[own_rows, :]) + bf16_product_t(rows, low_ref[own_rows, :])
        both = jnp.concatenate([solved[:, :strip], gram * gram - solved[:, strip:]], axis=1)
        out_ref[n, pl.ds(0, gathered), :] = both.astype(out_ref.dtype)

    for c in range(chunks):
        part = pl.ds(gathered + c * block, block)
        for p in column:
            pltpu.make_async_remote_copy(
                src_ref=made.at[p, pl.ds(c * block, block)],
                dst_ref=out_ref.at[p, part],
                send_sem=send_sem.at[c, 0],
                recv_sem=recv_sem.at[c, p],
                device_id=(w, p),
                device_id_type=MESH,
            ).wait_recv()
        kept[c].wait()
    for copy in copies:
        copy.wait_send()


def finish(rows, near, high, low, solve, upper, weight):
    strips, gathered, order = near.shape
    row_count = rows.shape[0]
    chunks = 2
    in_vmem = pl.BlockSpec(memory_space=pltpu.VMEM)
    width = P_SIZE // strips
    return pl.pallas_call(
        functools.partial(finish_kernel, strips, chunks),
        out_shape=jax.ShapeDtypeStruct((strips, gathered + row_count, width), jnp.bfloat16),
        in_specs=[in_vmem, pl.BlockSpec(memory_space=pl.ANY)] + [in_vmem] * 5,
        out_specs=in_vmem,
        scratch_shapes=[
            pltpu.VMEM((strips, row_count, width), jnp.bfloat16),
            pltpu.VMEM(near.shape, near.dtype),
            pltpu.SemaphoreType.DMA,
            pltpu.SemaphoreType.DMA((chunks,)),
            pltpu.SemaphoreType.DMA((chunks, strips - 1)),
            pltpu.SemaphoreType.DMA((chunks, strips)),
        ],
        compiler_params=pltpu.CompilerParams(
            collective_id=1, has_side_effects=True, vmem_limit_bytes=48 * 2**20
        ),
    )(rows, near, high, low, solve, upper, weight)


def local(constraint_rows, metric):
    n_wide, strips = lax.axis_size("wide"), lax.axis_size("narrow")
    groups = n_wide * strips
    depth = P_SIZE // groups
    ahead = DONE // groups
    order = metric.shape[0]
    own_rows = constraint_rows[:, 0, :]
    half = own_rows.shape[0] // 2
    near = lax.all_gather(own_rows[:half], "narrow", axis=0, tiled=False)
    gathered = gather_panel(own_rows[:depth], n_wide, strips)
    gathered = gathered.reshape(n_wide, strips, depth, order)
    first = gathered[:, :, :ahead].transpose(2, 0, 1, 3).reshape(DONE, order)
    rest = gathered[:, :, ahead:].transpose(1, 2, 0, 3).reshape(P_SIZE - DONE, order)
    panel = jnp.concatenate([first, rest], axis=0)
    solve, upper, weight, high, low = factor(panel, metric, strips)
    mine = finish(own_rows[half:], near, high, low, solve, upper, weight)
    return mine.astype(jnp.float32).transpose(1, 0, 2)[:, :, None, :]


def solution(mesh):
    placed = (P(None, ("wide", "narrow"), None), P())
    return jax.shard_map(
        local,
        mesh=mesh,
        in_specs=placed,
        out_specs=P(None, "wide", "narrow", None),
        check_vma=False,
    )
```
